32 devices in a mesh: dp: 16 (over z, x, core), tensor: 2 (over y).
Axes of the slice: x: 2, y: 2, z: 4, core: 2. Of those that a mesh axis runs over, the one named last changes fastest.
Arguments:
- inputs: bfloat16 [16384, 1024], P(('dp', 'tensor')), may hold values from -6 to 6
- norm1_gain: float32 [1024], replicated, may hold values from 0.5 to 1.5
- norm1_bias: float32 [1024], replicated, may hold values from -3 to 3
- qkv_weight: bfloat16 [1024, 3072], P('dp', 'tensor'), may hold values from -0.25 to 0.25
- qv_bias: float32 [2, 1024], P(None, 'tensor'), may hold values from -1.2 to 1.2
- out_weight: bfloat16 [1024, 1024], P('tensor', 'dp'), may hold values from -0.75 to 0.75
- out_bias: float32 [1024], replicated, may hold values from -3 to 3
- norm2_gain: float32 [1024], replicated, may hold values from 0.5 to 1.5
- norm2_bias: float32 [1024], replicated, may hold values from -3 to 3
- fc1_weight: bfloat16 [1024, 4096], P('dp', 'tensor'), may hold values from -0.1875 to 0.1875
- fc1_bias: float32 [4096], P('tensor'), may hold values from -3 to 3
- fc2_weight: bfloat16 [4096, 1024], P('tensor', 'dp'), may hold values from -0.09375 to 0.09375
- fc2_bias: float32 [1024], replicated, may hold values from -3 to 3
- cotangent: bfloat16 [16384, 1024], P(('dp', 'tensor')), may hold values from -6 to 6
Outputs:
- outputs: bfloat16 [16384, 1024], P(('dp', 'tensor'))
- grad_inputs: float32 [16384, 1024], P(('dp', 'tensor'))
- grad_norm1_gain: float32 [1024], replicated
- grad_norm1_bias: float32 [1024], replicated
- grad_qkv_weight: float32 [1024, 3072], P('dp', 'tensor')
- grad_qv_bias: float32 [2, 1024], P(None, 'tensor')
- grad_out_weight: float32 [1024, 1024], P('tensor', 'dp')
- grad_out_bias: float32 [1024], replicated
- grad_norm2_gain: float32 [1024], replicated
- grad_norm2_bias: float32 [1024], replicated
- grad_fc1_weight: float32 [1024, 4096], P('dp', 'tensor')
- grad_fc1_bias: float32 [4096], P('tensor')
- grad_fc2_weight: float32 [4096, 1024], P('tensor', 'dp')
- grad_fc2_bias: float32 [1024], replicated
The draws below stay inside these ranges and needn't reach their ends.
All inputs are finite; a program needn't handle non-finite values.
Results may differ from the reference program's by a relative error of at most 0.012.
The reference program's roundings to bfloat16 on the way count: a program that leaves them out, or rounds other values in their place, can miss the bound.
Values may be sent and summed in bfloat16 or wider, within the bound.
A program may use at most 192 MiB of HBM per device.

```python
import jax
import jax.numpy as jnp
from jax import lax

D = 1024
HEADS = 16
HD = 64
FF = 4096
LEN = 1024
SEQUENCES = 16
TOKENS = 16384


def shard_levels(rng, extent, pieces, low, top_value):
    level = 1.0
    for position, shards_of in pieces:
        heights = jax.random.uniform(jax.random.fold_in(jax.random.fold_in(rng, 6), position), (shards_of,), jnp.float32, low / len(pieces), top_value / len(pieces))
        level = level * jnp.repeat(jnp.exp(heights), extent[position] // shards_of).reshape((-1,) + (1,) * (len(extent) - 1 - position))
    return level


def gaussian(stream_key, dims, scale, bound, pieces=(), kind=jnp.bfloat16):
    values = jax.random.normal(stream_key, dims, jnp.float32) * scale
    if len(pieces) > 0:
        values = shard_levels(stream_key, dims, pieces, -0.22, 0.18) * values
    return jnp.clip(values, min=-bound, max=bound).astype(kind)


def setup_inputs(seed: int = 0) -> dict:
    streams_of = jax.random.split(jax.random.key(seed), 15)
    inputs = gaussian(streams_of[0], (TOKENS, D), 1.0, 6.0, ((0, 32),))
    norm1_gain = jnp.clip(jax.random.uniform(streams_of[1], (D,), jnp.float32, 0.5, 1.5), 0.5, 1.5)
    norm1_bias = gaussian(streams_of[2], (D,), 0.5, 3.0, (), jnp.float32)
    qkv_weight = gaussian(streams_of[3], (D, 3 * D), (D // 2) ** -0.5, 0.25, ((0, 16), (1, 2)))
    qv_bias = gaussian(streams_of[4], (2, D), 0.2, 1.2, ((1, 2),), jnp.float32)
    out_weight = gaussian(streams_of[5], (D, D), (D // 16) ** -0.5, 0.75, ((0, 2), (1, 16)))
    out_bias = gaussian(streams_of[6], (D,), 0.5, 3.0, (), jnp.float32)
    norm2_gain = jnp.clip(jax.random.uniform(streams_of[7], (D,), jnp.float32, 0.5, 1.5), 0.5, 1.5)
    norm2_bias = gaussian(streams_of[8], (D,), 0.5, 3.0, (), jnp.float32)
    fc1_weight = gaussian(streams_of[9], (D, FF), D ** -0.5, 0.1875, ((0, 16), (1, 2)))
    fc1_bias = gaussian(streams_of[10], (FF,), 0.5, 3.0, ((0, 2),), jnp.float32)
    fc2_weight = gaussian(streams_of[11], (FF, D), FF ** -0.5, 0.09375, ((0, 2), (1, 16)))
    fc2_bias = gaussian(streams_of[12], (D,), 0.5, 3.0, (), jnp.float32)
    cotangent = gaussian(streams_of[13], (TOKENS, D), 1.0, 6.0, ((0, 32),))
    return {"inputs": inputs, "norm1_gain": norm1_gain, "norm1_bias": norm1_bias, "qkv_weight": qkv_weight, "qv_bias": qv_bias, "out_weight": out_weight, "out_bias": out_bias, "norm2_gain": norm2_gain, "norm2_bias": norm2_bias, "fc1_weight": fc1_weight, "fc1_bias": fc1_bias, "fc2_weight": fc2_weight, "fc2_bias": fc2_bias, "cotangent": cotangent}


EPS = 1e-05
PRECISE = lax.Precision.HIGHEST

@jax.custom_vjp
def low(v):
    return lax.optimization_barrier(v.astype(jnp.bfloat16)).astype(jnp.float32)

@jax.custom_vjp
def low_back(v):
    return v

def low_keep(v):
    return (low(v), None)

def low_pass(kept, grad):
    return (grad,)

def back_keep(v):
    return (v, None)

def back_low(kept, grad):
    return (low(grad),)
low.defvjp(low_keep, low_pass)
low_back.defvjp(back_keep, back_low)

def layer_norm(values, gain, shift):
    center = values - lax.optimization_barrier(jnp.mean(values, -1, keepdims=True))
    spread = lax.optimization_barrier(jnp.mean(center * center, -1, keepdims=True))
    return center * lax.rsqrt(spread + EPS) * gain + shift

def attend_block(queries, keys, values, first_row):
    block_rows = queries.shape[0]
    scores = jnp.einsum('qhd,khd->hqk', queries, keys, precision=PRECISE) * HD ** (-0.5)
    scores = low_back(scores)
    query_pos = first_row + jnp.arange(block_rows, dtype=jnp.int32)
    key_pos = jnp.arange(keys.shape[0], dtype=jnp.int32)
    allowed = key_pos[None, :] <= query_pos[:, None]
    scores = jnp.where(allowed[None], scores, -1e+30)
    row_max = lax.optimization_barrier(jnp.max(scores, -1, keepdims=True))
    expo = jnp.exp(scores - row_max)
    probs = expo / lax.optimization_barrier(jnp.sum(expo, -1, keepdims=True))
    return jnp.einsum('hqk,khd->qhd', low(probs), values, precision=PRECISE)

def layer_forward(seq_inputs, params):
    norm1_gain, norm1_bias, qkv_weight, qv_bias, out_weight, out_bias, norm2_gain, norm2_bias, fc1_weight, fc1_bias, fc2_weight, fc2_bias = params
    normed1 = low(layer_norm(seq_inputs, norm1_gain, norm1_bias))
    no_bias = jnp.zeros((HEADS, HD), jnp.float32)
    full_bias = jnp.stack([qv_bias[0].reshape(HEADS, HD), no_bias, qv_bias[1].reshape(HEADS, HD)], 1).reshape(3 * D)
    qkv = jnp.dot(normed1, qkv_weight, precision=PRECISE) + full_bias
    qkv = low_back(low(qkv)).reshape(LEN, HEADS, 3, HD)
    queries, keys, values = (qkv[:, :, 0], qkv[:, :, 1], qkv[:, :, 2])
    block_rows = min(512, LEN)
    blocks = LEN // block_rows
    query_blocks = queries.reshape(blocks, block_rows, HEADS, HD)
    starts = jnp.arange(blocks, dtype=jnp.int32) * block_rows
    block_fn = jax.checkpoint(lambda operand: attend_block(operand[0], keys, values, operand[1]))
    context = lax.map(block_fn, (query_blocks, starts)).reshape(LEN, D)
    context = low_back(low(context))
    attn = low_back(jnp.dot(context, out_weight, precision=PRECISE))
    mid = seq_inputs + attn + out_bias
    normed2 = low(layer_norm(mid, norm2_gain, norm2_bias))
    pre = low_back(jnp.dot(normed2, fc1_weight, precision=PRECISE) + fc1_bias)
    act = low(jax.nn.gelu(pre, approximate=True))
    branch = low_back(jnp.dot(act, fc2_weight, precision=PRECISE))
    return mid + branch + fc2_bias

def reference(inputs, norm1_gain, norm1_bias, qkv_weight, qv_bias, out_weight, out_bias, norm2_gain, norm2_bias, fc1_weight, fc1_bias, fc2_weight, fc2_bias, cotangent):
    params = tuple((param.astype(jnp.float32) for param in (norm1_gain, norm1_bias, qkv_weight, qv_bias, out_weight, out_bias, norm2_gain, norm2_bias, fc1_weight, fc1_bias, fc2_weight, fc2_bias)))
    seq_inputs = inputs.astype(jnp.float32).reshape(SEQUENCES, LEN, D)
    seq_grads = cotangent.astype(jnp.float32).reshape(SEQUENCES, LEN, D)

    def one_sequence(totals, operand):
        result, pull = jax.vjp(layer_forward, operand[0], params)
        grad_in, grad_params = pull(operand[1])
        totals = jax.tree.map(lambda first, second: first + second, totals, grad_params)
        return (totals, (result.astype(jnp.bfloat16), grad_in))
    start_totals = tuple((jnp.zeros_like(param) for param in params))
    totals, (results, grad_ins) = lax.scan(one_sequence, start_totals, (seq_inputs, seq_grads))
    return (results.reshape(TOKENS, D), grad_ins.reshape(TOKENS, D), totals[0], totals[1], totals[2], totals[3], totals[4], totals[5], totals[6], totals[7], totals[8], totals[9], totals[10], totals[11])
```

```python
from functools import partial

import jax
import jax.numpy as jnp
from jax import lax
from jax.experimental import pallas as pl
from jax.experimental.pallas import tpu as pltpu
from jax.sharding import Mesh
from jax.sharding import PartitionSpec as P

D = 1024
HD = 64
FF = 4096
LEN = 1024
SEQS = 1


EPS = 1e-05


def layer_norm(values, gain, shift):
    center = values - jnp.mean(values, -1, keepdims=True)
    spread = jnp.mean(center * center, -1, keepdims=True)
    return center * lax.rsqrt(spread + EPS) * gain + shift


def masked_scores(query_block, keys, first_row, factor):
    block_rows = query_block.shape[0]
    scores = (
        jnp.einsum("qhd,khd->hqk", query_block, keys, preferred_element_type=jnp.float32) * factor
    )
    query_pos = first_row + jnp.arange(block_rows, dtype=jnp.int32)
    key_pos = jnp.arange(keys.shape[0], dtype=jnp.int32)
    allowed = key_pos[None, :] <= query_pos[:, None]
    return jnp.where(allowed[None], scores, -1e30)


def attention_forward(queries, keys, values, factor):
    length = queries.shape[0]
    block_rows = min(512, length)
    block_count = length // block_rows

    def one_block(block_index):
        first_row = block_index * block_rows
        query_block = lax.dynamic_slice_in_dim(queries, first_row, block_rows, 0)
        scores = masked_scores(query_block, keys, first_row, factor)
        row_max = jnp.max(scores, -1, keepdims=True)
        expo = jnp.exp(scores - row_max)
        exp_total = jnp.sum(expo, -1, keepdims=True)
        probs_low = (expo / exp_total).astype(jnp.bfloat16)
        context = jnp.einsum("hqk,khd->qhd", probs_low, values, preferred_element_type=jnp.float32)
        return (context.astype(jnp.bfloat16), (row_max + jnp.log(exp_total))[..., 0])

    context, log_total = lax.map(one_block, jnp.arange(block_count, dtype=jnp.int32))
    return (context.reshape(queries.shape), log_total)


def attention_backward(queries, keys, values, log_total, grad_context, factor):
    length = queries.shape[0]
    block_rows = min(512, length)
    block_count = length // block_rows

    def one_block(carry, block_index):
        grad_keys, grad_values = carry
        first_row = block_index * block_rows
        query_block = lax.dynamic_slice_in_dim(queries, first_row, block_rows, 0)
        grad_block = lax.dynamic_slice_in_dim(grad_context, first_row, block_rows, 0)
        scores = masked_scores(query_block, keys, first_row, factor)
        probs = jnp.exp(scores - log_total[block_index][..., None])
        probs_low = probs.astype(jnp.bfloat16)
        grad_values = grad_values + jnp.einsum(
            "hqk,qhd->khd", probs_low, grad_block, preferred_element_type=jnp.float32
        )
        grad_probs = jnp.einsum(
            "qhd,khd->hqk", grad_block, values, preferred_element_type=jnp.float32
        )
        grad_scores = probs * (grad_probs - jnp.sum(probs * grad_probs, -1, keepdims=True))
        grad_scores = grad_scores.astype(jnp.bfloat16)
        grad_query = (
            jnp.einsum("hqk,khd->qhd", grad_scores, keys, preferred_element_type=jnp.float32)
            * factor
        )
        grad_keys = (
            grad_keys
            + jnp.einsum(
                "hqk,qhd->khd", grad_scores, query_block, preferred_element_type=jnp.float32
            )
            * factor
        )
        return ((grad_keys, grad_values), grad_query.astype(jnp.bfloat16))

    start_carry = (jnp.zeros(keys.shape, jnp.float32), jnp.zeros(values.shape, jnp.float32))
    (grad_keys, grad_values), grad_queries = lax.scan(
        one_block, start_carry, jnp.arange(block_count, dtype=jnp.int32)
    )
    return (
        grad_queries.reshape(queries.shape),
        grad_keys.astype(jnp.bfloat16),
        grad_values.astype(jnp.bfloat16),
    )


def row_product(left_rows, right_mat):
    return jnp.dot(left_rows, right_mat, preferred_element_type=jnp.float32)


def row_product_back(left_rows, right_mat):
    return jnp.einsum("rc,dc->rd", left_rows, right_mat, preferred_element_type=jnp.float32)


def body(
    inputs,
    norm1_gain,
    norm1_bias,
    qkv_weight,
    qv_bias,
    out_weight,
    out_bias,
    norm2_gain,
    norm2_bias,
    fc1_weight,
    fc1_bias,
    fc2_weight,
    fc2_bias,
    cotangent,
):
    width_here = qv_bias.shape[1]
    heads_here = width_here // HD
    hidden_here = fc1_bias.shape[0]
    factor = HD ** (-0.5)
    inputs_f = inputs.astype(jnp.float32)
    tensor_index = lax.axis_index("tensor")
    qkv_full, out_full, fc1_full, fc2_full = (
        lax.all_gather(qkv_weight, "dp", axis=0, tiled=True),
        lax.all_gather(out_weight, "dp", axis=1, tiled=True),
        lax.all_gather(fc1_weight, "dp", axis=0, tiled=True),
        lax.all_gather(fc2_weight, "dp", axis=1, tiled=True),
    )
    normed1 = lax.all_gather(
        layer_norm(inputs_f, norm1_gain, norm1_bias).astype(jnp.bfloat16),
        "tensor",
        axis=0,
        tiled=True,
    )
    total_rows = normed1.shape[0]
    no_bias = jnp.zeros((heads_here, HD), jnp.float32)
    head_bias = jnp.stack(
        [qv_bias[0].reshape(heads_here, HD), no_bias, qv_bias[1].reshape(heads_here, HD)], 1
    )
    projected = (
        jnp.dot(normed1, qkv_full, preferred_element_type=jnp.float32).reshape(
            total_rows, heads_here, 3, HD
        )
        + head_bias
    )
    projected = projected.astype(jnp.bfloat16).reshape(SEQS, LEN, heads_here, 3, HD)
    queries = projected[:, :, :, 0]
    keys = projected[:, :, :, 1]
    values = projected[:, :, :, 2]
    context, log_total = lax.map(
        lambda operand: attention_forward(operand[0], operand[1], operand[2], factor),
        (queries, keys, values),
    )
    context = context.reshape(total_rows, width_here)
    attn_part = lax.psum_scatter(
        row_product(context, out_full), "tensor", scatter_dimension=0, tiled=True
    )
    middle = inputs_f + attn_part + out_bias
    normed2 = lax.all_gather(
        layer_norm(middle, norm2_gain, norm2_bias).astype(jnp.bfloat16),
        "tensor",
        axis=0,
        tiled=True,
    )
    pre_act = jnp.dot(normed2, fc1_full, preferred_element_type=jnp.float32) + fc1_bias
    activ = jax.nn.gelu(pre_act, approximate=True).astype(jnp.bfloat16)
    branch = lax.psum_scatter(
        row_product(activ, fc2_full).astype(jnp.bfloat16), "tensor", scatter_dimension=0, tiled=True
    ).astype(jnp.float32)
    outputs = (middle + branch + fc2_bias).astype(jnp.bfloat16)
    qkv_back, out_back, fc1_back, fc2_back = (
        lax.all_gather(qkv_weight, "dp", axis=0, tiled=True),
        lax.all_gather(out_weight, "dp", axis=1, tiled=True),
        lax.all_gather(fc1_weight, "dp", axis=0, tiled=True),
        lax.all_gather(fc2_weight, "dp", axis=1, tiled=True),
    )
    grad_outputs = cotangent.astype(jnp.float32)
    grad_branch = lax.all_gather(cotangent, "tensor", axis=0, tiled=True)
    grad_activ = jnp.einsum("rd,fd->rf", grad_branch, fc2_back, preferred_element_type=jnp.float32)
    grad_fc2 = jnp.einsum("rf,rd->fd", activ, grad_branch, preferred_element_type=jnp.float32)
    gelu_pull = jax.vjp(partial(jax.nn.gelu, approximate=True), pre_act)[1]
    grad_pre = gelu_pull(grad_activ)[0].astype(jnp.bfloat16)
    grad_fc1_b = jnp.sum(grad_pre.astype(jnp.float32), 0)
    grad_fc1 = jnp.einsum("rd,rf->df", normed2, grad_pre, preferred_element_type=jnp.float32)
    grad_normed2 = lax.psum_scatter(
        row_product_back(grad_pre, fc1_back), "tensor", scatter_dimension=0, tiled=True
    )
    norm2_pull = jax.vjp(layer_norm, middle, norm2_gain, norm2_bias)[1]
    grad_mid_norm, grad_gain2, grad_shift2 = norm2_pull(grad_normed2)
    grad_middle = grad_outputs + grad_mid_norm
    grad_attn = lax.all_gather(grad_middle.astype(jnp.bfloat16), "tensor", axis=0, tiled=True)
    grad_ctx = jnp.einsum(
        "rd,cd->rc", grad_attn, out_back, preferred_element_type=jnp.float32
    ).astype(jnp.bfloat16)
    grad_out_w = jnp.einsum("rc,rd->cd", context, grad_attn, preferred_element_type=jnp.float32)
    grad_queries, grad_keys, grad_values = lax.map(
        lambda operand: attention_backward(
            operand[0], operand[1], operand[2], operand[3], operand[4], factor
        ),
        (queries, keys, values, log_total, grad_ctx.reshape(SEQS, LEN, heads_here, HD)),
    )
    grad_proj = jnp.stack([grad_queries, grad_keys, grad_values], 3).reshape(
        total_rows, 3 * width_here
    )
    grad_qv_here = jnp.stack(
        [
            jnp.sum(grad_queries.astype(jnp.float32), (0, 1)).reshape(width_here),
            jnp.sum(grad_values.astype(jnp.float32), (0, 1)).reshape(width_here),
        ]
    )
    grad_qkv_w = jnp.einsum("rd,rc->dc", normed1, grad_proj, preferred_element_type=jnp.float32)
    grad_normed1 = lax.psum_scatter(
        row_product_back(grad_proj, qkv_back), "tensor", scatter_dimension=0, tiled=True
    )
    norm1_pull = jax.vjp(layer_norm, inputs_f, norm1_gain, norm1_bias)[1]
    grad_in_norm, grad_gain1, grad_shift1 = norm1_pull(grad_normed1)
    grad_inputs = grad_middle + grad_in_norm
    grad_qkv_s, grad_out_s, grad_fc1_s, grad_fc2_s = (
        lax.psum_scatter(grad_qkv_w, "dp", scatter_dimension=0, tiled=True),
        lax.psum_scatter(grad_out_w, "dp", scatter_dimension=1, tiled=True),
        lax.psum_scatter(grad_fc1, "dp", scatter_dimension=0, tiled=True),
        lax.psum_scatter(grad_fc2, "dp", scatter_dimension=1, tiled=True),
    )
    vector_terms = jnp.stack(
        [
            grad_gain1,
            grad_shift1,
            grad_gain2,
            grad_shift2,
            jnp.sum(grad_middle, 0),
            jnp.sum(grad_outputs, 0),
        ]
    )
    qv_whole = lax.dynamic_update_slice_in_dim(
        jnp.zeros((2, D), jnp.float32), grad_qv_here, tensor_index * width_here, 1
    )
    fc1_whole = lax.dynamic_update_slice_in_dim(
        jnp.zeros((FF,), jnp.float32), grad_fc1_b, tensor_index * hidden_here, 0
    )
    vector_sum, qv_sum, fc1_sum = lax.psum((vector_terms, qv_whole, fc1_whole), ("dp", "tensor"))
    grad_qv = lax.dynamic_slice_in_dim(qv_sum, tensor_index * width_here, width_here, 1)
    grad_fc1_bias = lax.dynamic_slice_in_dim(fc1_sum, tensor_index * hidden_here, hidden_here, 0)
    return (
        outputs,
        grad_inputs,
        vector_sum[0],
        vector_sum[1],
        grad_qkv_s,
        grad_qv,
        grad_out_s,
        vector_sum[4],
        vector_sum[2],
        vector_sum[3],
        grad_fc1_s,
        grad_fc1_bias,
        grad_fc2_s,
        vector_sum[5],
    )


ALL = ("zx", "core", "tensor")
GROUP = ("zx", "tensor")
NEG = -1e30


def natural_rows(ref, first, second, half):
    return jnp.concatenate([ref[pl.ds(first, half), :], ref[pl.ds(second, half), :]], 0)


def half_offsets(index_ref, half):
    index = index_ref[0]
    return pl.multiple_of(index * half, half), pl.multiple_of((1 - index) * half, half)


def dot_nt(left, right):
    return lax.dot_general(left, right, (((1,), (1,)), ((), ())), preferred_element_type=jnp.float32)


def dot_tn(left, right):
    return lax.dot_general(left, right, (((0,), (0,)), ((), ())), preferred_element_type=jnp.float32)


def block_probs(query_rows, keys, block):
    scores = dot_nt(query_rows, keys)
    before = keys.shape[0] - block
    rows = lax.broadcasted_iota(jnp.int32, (block, block), 0)
    columns = lax.broadcasted_iota(jnp.int32, (block, block), 1)
    diagonal = jnp.where(columns <= rows, scores[:, before:], NEG)
    if before:
        scores = jnp.concatenate([scores[:, :before], diagonal], 1)
    else:
        scores = diagonal
    expo = jnp.exp(scores - jnp.max(scores, -1, keepdims=True))
    return expo * (1.0 / jnp.sum(expo, -1, keepdims=True))


def attend_kernel(index_ref, qkv_ref, context_ref):
    half = qkv_ref.shape[0] // 2
    block = half // 2
    first, second = half_offsets(index_ref, half)
    qkv = natural_rows(qkv_ref, first, second, half)
    heads = qkv.shape[1] // (3 * HD)
    for i in range(4):
        row = (first if i < 2 else second) + (i % 2) * block
        parts = []
        for h in range(heads):
            base = h * 3 * HD
            query_rows = qkv[i * block : (i + 1) * block, base : base + HD] * HD ** (-0.5)
            keys = qkv[: (i + 1) * block, base + HD : base + 2 * HD]
            values = qkv[: (i + 1) * block, base + 2 * HD : base + 3 * HD]
            probs = block_probs(query_rows.astype(jnp.bfloat16), keys, block)
            parts.append(
                jnp.dot(probs.astype(jnp.bfloat16), values, preferred_element_type=jnp.float32)
            )
        context_ref[pl.ds(pl.multiple_of(row, block), block), :] = jnp.concatenate(
            parts, 1
        ).astype(jnp.bfloat16)


def attend_back_kernel(index_ref, qkv_ref, grad_ref, out_ref):
    half = qkv_ref.shape[0] // 2
    block = half // 2
    first, second = half_offsets(index_ref, half)
    qkv = natural_rows(qkv_ref, first, second, half)
    grad = natural_rows(grad_ref, first, second, half)
    heads = qkv.shape[1] // (3 * HD)
    starts = [
        pl.multiple_of((first if i < 2 else second) + (i % 2) * block, block) for i in range(4)
    ]
    for h in range(heads):
        base = h * 3 * HD
        queries = (qkv[:, base : base + HD] * HD ** (-0.5)).astype(jnp.bfloat16)
        keys = qkv[:, base + HD : base + 2 * HD]
        values = qkv[:, base + 2 * HD : base + 3 * HD]
        grad_head = grad[:, h * HD : (h + 1) * HD]
        grad_keys = [None] * 4
        grad_values = [None] * 4
        for i in range(4):
            rows = slice(i * block, (i + 1) * block)
            seen = slice(0, (i + 1) * block)
            probs = block_probs(queries[rows], keys[seen], block)
            grad_probs = dot_nt(grad_head[rows], values[seen])
            inner = jnp.sum(probs * grad_probs, -1, keepdims=True)
            grad_scores = (probs * (grad_probs - inner)).astype(jnp.bfloat16)
            grad_query = jnp.dot(grad_scores, keys[seen], preferred_element_type=jnp.float32)
            out_ref[pl.ds(starts[i], block), base : base + HD] = (
                grad_query * HD ** (-0.5)
            ).astype(jnp.bfloat16)
            key_term = dot_tn(grad_scores, queries[rows])
            value_term = dot_tn(probs.astype(jnp.bfloat16), grad_head[rows])
            for j in range(i + 1):
                key_part = key_term[j * block : (j + 1) * block]
                value_part = value_term[j * block : (j + 1) * block]
                grad_keys[j] = key_part if i == j else grad_keys[j] + key_part
                grad_values[j] = value_part if i == j else grad_values[j] + value_part
        for j in range(4):
            out_ref[pl.ds(starts[j], block), base + HD : base + 3 * HD] = jnp.concatenate(
                [grad_keys[j], grad_values[j]], 1
            ).astype(jnp.bfloat16)


def attend(index, qkv):
    rows, width = qkv.shape
    pairs = width // (6 * HD)
    return pl.pallas_call(
        attend_kernel,
        grid=(pairs,),
        in_specs=[
            pl.BlockSpec(memory_space=pltpu.SMEM),
            pl.BlockSpec((rows, 6 * HD), lambda i: (0, i)),
        ],
        out_specs=pl.BlockSpec((rows, 2 * HD), lambda i: (0, i)),
        out_shape=jax.ShapeDtypeStruct((rows, width // 3), jnp.bfloat16),
        compiler_params=pltpu.CompilerParams(vmem_limit_bytes=40 << 20),
        cost_estimate=pl.CostEstimate(
            flops=pairs * 8 * HD * rows * rows,
            bytes_accessed=8 * rows * width // 3,
            transcendentals=pairs * 2 * rows * rows,
        ),
    )(index, qkv)


def attend_back(index, qkv, grad):
    rows, width = qkv.shape
    pairs = width // (6 * HD)
    return pl.pallas_call(
        attend_back_kernel,
        grid=(pairs,),
        in_specs=[
            pl.BlockSpec(memory_space=pltpu.SMEM),
            pl.BlockSpec((rows, 6 * HD), lambda i: (0, i)),
            pl.BlockSpec((rows, 2 * HD), lambda i: (0, i)),
        ],
        out_specs=pl.BlockSpec((rows, 6 * HD), lambda i: (0, i)),
        out_shape=jax.ShapeDtypeStruct((rows, width), jnp.bfloat16),
        compiler_params=pltpu.CompilerParams(vmem_limit_bytes=40 << 20),
        cost_estimate=pl.CostEstimate(
            flops=pairs * 20 * HD * rows * rows,
            bytes_accessed=14 * rows * width // 3,
            transcendentals=pairs * 2 * rows * rows,
        ),
    )(index, qkv, grad)


def pair_body(
    zx_size,
    inputs,
    norm1_gain,
    norm1_bias,
    qkv_weight,
    qv_bias,
    out_weight,
    out_bias,
    norm2_gain,
    norm2_bias,
    fc1_weight,
    fc1_bias,
    fc2_weight,
    fc2_bias,
    cotangent,
):
    f32, bf16 = jnp.float32, jnp.bfloat16
    crossing = [
        (z * 4 + c * 2 + t, z * 4 + t * 2 + c)
        for z in range(zx_size)
        for c in range(2)
        for t in range(2)
    ]

    def swap(value):
        return lax.ppermute(value, ALL, crossing)

    def flip(value):
        return lax.ppermute(value, "core", [(0, 1), (1, 0)])

    def both(own):
        return jnp.concatenate([own, flip(own)], 0)

    def pair_sum(product, rows):
        half = rows.shape[0] // 2
        arrived = flip(product(rows[half:]).astype(bf16))
        return product(rows[:half]) + arrived.astype(f32)

    def gather(weight, axis):
        return lax.all_gather(weight, GROUP, axis=axis, tiled=True)

    def scatter(grad, axis):
        return lax.psum_scatter(grad.astype(bf16), GROUP, scatter_dimension=axis, tiled=True)

    inputs = swap(inputs)
    qkv_full = gather(swap(qkv_weight), 0)
    qv_bias = swap(qv_bias)
    fc1_bias = swap(fc1_bias)
    out_full = gather(swap(out_weight), 1)
    fc1_full = gather(swap(fc1_weight), 0)
    fc2_full = gather(swap(fc2_weight), 1)
    cotangent = swap(cotangent)

    width_here = qv_bias.shape[1]
    heads_here = width_here // HD
    inputs_f = inputs.astype(f32)
    index = lax.axis_index("core").astype(jnp.int32).reshape(1)
    normed1 = both(layer_norm(inputs_f, norm1_gain, norm1_bias).astype(bf16))
    head_bias = jnp.stack(
        [
            qv_bias[0].reshape(heads_here, HD),
            jnp.zeros((heads_here, HD), f32),
            qv_bias[1].reshape(heads_here, HD),
        ],
        1,
    ).reshape(3 * width_here)
    qkv = (row_product(normed1, qkv_full) + head_bias).astype(bf16)
    context = attend(index, qkv)
    middle = inputs_f + pair_sum(lambda rows: row_product(rows, out_full), context) + out_bias
    normed2 = both(layer_norm(middle, norm2_gain, norm2_bias).astype(bf16))
    pre_act = row_product(normed2, fc1_full) + fc1_bias
    activ = jax.nn.gelu(pre_act, approximate=True).astype(bf16)
    branch = pair_sum(lambda rows: row_product(rows, fc2_full), activ)
    outputs = swap((middle + branch + fc2_bias).astype(bf16))

    grad_outputs = cotangent.astype(f32)
    grad_branch = both(cotangent)
    grad_fc2 = swap(
        scatter(jnp.einsum("rf,rd->fd", activ, grad_branch, preferred_element_type=f32), 1)
    ).astype(f32)
    grad_activ = row_product_back(grad_branch, fc2_full)
    gelu_pull = jax.vjp(partial(jax.nn.gelu, approximate=True), pre_act)[1]
    grad_pre = gelu_pull(grad_activ)[0].astype(bf16)
    grad_fc1_b = jnp.sum(grad_pre.astype(f32), 0)
    grad_fc1 = swap(
        scatter(jnp.einsum("rd,rf->df", normed2, grad_pre, preferred_element_type=f32), 0)
    ).astype(f32)
    grad_normed2 = pair_sum(lambda rows: row_product_back(rows, fc1_full), grad_pre)
    norm2_pull = jax.vjp(layer_norm, middle, norm2_gain, norm2_bias)[1]
    grad_mid_norm, grad_gain2, grad_shift2 = norm2_pull(grad_normed2)
    grad_middle = grad_outputs + grad_mid_norm
    grad_attn = both(grad_middle.astype(bf16))
    grad_ctx = row_product_back(grad_attn, out_full).astype(bf16)
    grad_out = swap(
        scatter(jnp.einsum("rc,rd->cd", context, grad_attn, preferred_element_type=f32), 1)
    ).astype(f32)
    grad_proj = attend_back(index, qkv, grad_ctx)
    grad_bias = jnp.sum(grad_proj.astype(f32), 0).reshape(heads_here, 3, HD)
    grad_qkv = swap(
        scatter(jnp.einsum("rd,rc->dc", normed1, grad_proj, preferred_element_type=f32), 0)
    ).astype(f32)
    grad_normed1 = pair_sum(lambda rows: row_product_back(rows, qkv_full), grad_proj)
    norm1_pull = jax.vjp(layer_norm, inputs_f, norm1_gain, norm1_bias)[1]
    grad_in_norm, grad_gain1, grad_shift1 = norm1_pull(grad_normed1)
    grad_inputs = swap((grad_middle + grad_in_norm).astype(bf16)).astype(f32)

    vectors = [
        grad_gain1,
        grad_shift1,
        grad_gain2,
        grad_shift2,
        jnp.sum(grad_middle, 0),
        jnp.sum(grad_outputs, 0),
    ]
    width = inputs.shape[1]
    hidden = grad_fc1_b.shape[0]
    terms = jnp.concatenate(
        vectors + [grad_bias[:, 0].reshape(-1), grad_bias[:, 2].reshape(-1), grad_fc1_b]
    )
    gathered = lax.all_gather(terms, ALL, axis=0, tiled=False)
    gathered = gathered.reshape(zx_size, 2, 2, terms.shape[0])
    common = jnp.sum(gathered[..., : 6 * width], (0, 1, 2)).reshape(6, width)
    halves = jnp.sum(gathered[..., 6 * width :], (0, 2))
    mine = lax.dynamic_index_in_dim(halves, lax.axis_index("tensor"), 0, False)
    return (
        outputs,
        grad_inputs,
        common[0],
        common[1],
        grad_qkv,
        mine[: 2 * width_here].reshape(2, width_here),
        grad_out,
        common[4],
        common[2],
        common[3],
        grad_fc1,
        mine[2 * width_here : 2 * width_here + hidden],
        grad_fc2,
        common[5],
    )


def pair_solution(mesh):
    zx_size = mesh.shape["dp"] // 2
    split = Mesh(mesh.devices.reshape(zx_size, 2, 2), ALL)
    rows, spread = P(ALL, None), ("zx", "core")
    return jax.shard_map(
        partial(pair_body, zx_size),
        mesh=split,
        in_specs=(
            rows,
            P(),
            P(),
            P(spread, "tensor"),
            P(None, "tensor"),
            P("tensor", spread),
            P(),
            P(),
            P(),
            P(spread, "tensor"),
            P("tensor"),
            P("tensor", spread),
            P(),
            rows,
        ),
        out_specs=(
            rows,
            rows,
            P(),
            P(),
            P(spread, "tensor"),
            P(None, "tensor"),
            P("tensor", spread),
            P(),
            P(),
            P(),
            P(spread, "tensor"),
            P("tensor"),
            P("tensor", spread),
            P(),
        ),
        check_vma=False,
    )


def solution(mesh):
    if mesh.shape["tensor"] == 2 and mesh.shape["dp"] % 2 == 0:
        return pair_solution(mesh)
    placed = (
        P(("dp", "tensor"), None),
        P(),
        P(),
        P("dp", "tensor"),
        P(None, "tensor"),
        P("tensor", "dp"),
        P(),
        P(),
        P(),
        P("dp", "tensor"),
        P("tensor"),
        P("tensor", "dp"),
        P(),
        P(("dp", "tensor"), None),
    )
    return jax.shard_map(
        body,
        mesh=mesh,
        in_specs=placed,
        out_specs=(
            P(("dp", "tensor"), None),
            P(("dp", "tensor"), None),
            P(),
            P(),
            P("dp", "tensor"),
            P(None, "tensor"),
            P("tensor", "dp"),
            P(),
            P(),
            P(),
            P("dp", "tensor"),
            P("tensor"),
            P("tensor", "dp"),
            P(),
        ),
        check_vma=False,
    )
```

```python
from functools import partial

import jax
import jax.numpy as jnp
from jax import lax
from jax.experimental import pallas as pl
from jax.experimental.pallas import tpu as pltpu
from jax.sharding import Mesh
from jax.sharding import PartitionSpec as P

D = 1024
HD = 64
FF = 4096
LEN = 1024
SEQS = 1


EPS = 1e-05


def layer_norm(values, gain, shift):
    center = values - jnp.mean(values, -1, keepdims=True)
    spread = jnp.mean(center * center, -1, keepdims=True)
    return center * lax.rsqrt(spread + EPS) * gain + shift


def masked_scores(query_block, keys, first_row, factor):
    block_rows = query_block.shape[0]
    scores = (
        jnp.einsum("qhd,khd->hqk", query_block, keys, preferred_element_type=jnp.float32) * factor
    )
    query_pos = first_row + jnp.arange(block_rows, dtype=jnp.int32)
    key_pos = jnp.arange(keys.shape[0], dtype=jnp.int32)
    allowed = key_pos[None, :] <= query_pos[:, None]
    return jnp.where(allowed[None], scores, -1e30)


def attention_forward(queries, keys, values, factor):
    length = queries.shape[0]
    block_rows = min(512, length)
    block_count = length // block_rows

    def one_block(block_index):
        first_row = block_index * block_rows
        query_block = lax.dynamic_slice_in_dim(queries, first_row, block_rows, 0)
        scores = masked_scores(query_block, keys, first_row, factor)
        row_max = jnp.max(scores, -1, keepdims=True)
        expo = jnp.exp(scores - row_max)
        exp_total = jnp.sum(expo, -1, keepdims=True)
        probs_low = (expo / exp_total).astype(jnp.bfloat16)
        context = jnp.einsum("hqk,khd->qhd", probs_low, values, preferred_element_type=jnp.float32)
        return (context.astype(jnp.bfloat16), (row_max + jnp.log(exp_total))[..., 0])

    context, log_total = lax.map(one_block, jnp.arange(block_count, dtype=jnp.int32))
    return (context.reshape(queries.shape), log_total)


def attention_backward(queries, keys, values, log_total, grad_context, factor):
    length = queries.shape[0]
    block_rows = min(512, length)
    block_count = length // block_rows

    def one_block(carry, block_index):
        grad_keys, grad_values = carry
        first_row = block_index * block_rows
        query_block = lax.dynamic_slice_in_dim(queries, first_row, block_rows, 0)
        grad_block = lax.dynamic_slice_in_dim(grad_context, first_row, block_rows, 0)
        scores = masked_scores(query_block, keys, first_row, factor)
        probs = jnp.exp(scores - log_total[block_index][..., None])
        probs_low = probs.astype(jnp.bfloat16)
        grad_values = grad_values + jnp.einsum(
            "hqk,qhd->khd", probs_low, grad_block, preferred_element_type=jnp.float32
        )
        grad_probs = jnp.einsum(
            "qhd,khd->hqk", grad_block, values, preferred_element_type=jnp.float32
        )
        grad_scores = probs * (grad_probs - jnp.sum(probs * grad_probs, -1, keepdims=True))
        grad_scores = grad_scores.astype(jnp.bfloat16)
        grad_query = (
            jnp.einsum("hqk,khd->qhd", grad_scores, keys, preferred_element_type=jnp.float32)
            * factor
        )
        grad_keys = (
            grad_keys
            + jnp.einsum(
                "hqk,qhd->khd", grad_scores, query_block, preferred_element_type=jnp.float32
            )
            * factor
        )
        return ((grad_keys, grad_values), grad_query.astype(jnp.bfloat16))

    start_carry = (jnp.zeros(keys.shape, jnp.float32), jnp.zeros(values.shape, jnp.float32))
    (grad_keys, grad_values), grad_queries = lax.scan(
        one_block, start_carry, jnp.arange(block_count, dtype=jnp.int32)
    )
    return (
        grad_queries.reshape(queries.shape),
        grad_keys.astype(jnp.bfloat16),
        grad_values.astype(jnp.bfloat16),
    )


def row_product(left_rows, right_mat):
    return jnp.dot(left_rows, right_mat, preferred_element_type=jnp.float32)


def row_product_back(left_rows, right_mat):
    return jnp.einsum("rc,dc->rd", left_rows, right_mat, preferred_element_type=jnp.float32)


def body(
    inputs,
    norm1_gain,
    norm1_bias,
    qkv_weight,
    qv_bias,
    out_weight,
    out_bias,
    norm2_gain,
    norm2_bias,
    fc1_weight,
    fc1_bias,
    fc2_weight,
    fc2_bias,
    cotangent,
):
    width_here = qv_bias.shape[1]
    heads_here = width_here // HD
    hidden_here = fc1_bias.shape[0]
    factor = HD ** (-0.5)
    inputs_f = inputs.astype(jnp.float32)
    tensor_index = lax.axis_index("tensor")
    qkv_full, out_full, fc1_full, fc2_full = (
        lax.all_gather(qkv_weight, "dp", axis=0, tiled=True),
        lax.all_gather(out_weight, "dp", axis=1, tiled=True),
        lax.all_gather(fc1_weight, "dp", axis=0, tiled=True),
        lax.all_gather(fc2_weight, "dp", axis=1, tiled=True),
    )
    normed1 = lax.all_gather(
        layer_norm(inputs_f, norm1_gain, norm1_bias).astype(jnp.bfloat16),
        "tensor",
        axis=0,
        tiled=True,
    )
    total_rows = normed1.shape[0]
    no_bias = jnp.zeros((heads_here, HD), jnp.float32)
    head_bias = jnp.stack(
        [qv_bias[0].reshape(heads_here, HD), no_bias, qv_bias[1].reshape(heads_here, HD)], 1
    )
    projected = (
        jnp.dot(normed1, qkv_full, preferred_element_type=jnp.float32).reshape(
            total_rows, heads_here, 3, HD
        )
        + head_bias
    )
    projected = projected.astype(jnp.bfloat16).reshape(SEQS, LEN, heads_here, 3, HD)
    queries = projected[:, :, :, 0]
    keys = projected[:, :, :, 1]
    values = projected[:, :, :, 2]
    context, log_total = lax.map(
        lambda operand: attention_forward(operand[0], operand[1], operand[2], factor),
        (queries, keys, values),
    )
    context = context.reshape(total_rows, width_here)
    attn_part = lax.psum_scatter(
        row_product(context, out_full), "tensor", scatter_dimension=0, tiled=True
    )
    middle = inputs_f + attn_part + out_bias
    normed2 = lax.all_gather(
        layer_norm(middle, norm2_gain, norm2_bias).astype(jnp.bfloat16),
        "tensor",
        axis=0,
        tiled=True,
    )
    pre_act = jnp.dot(normed2, fc1_full, preferred_element_type=jnp.float32) + fc1_bias
    activ = jax.nn.gelu(pre_act, approximate=True).astype(jnp.bfloat16)
    branch = lax.psum_scatter(
        row_product(activ, fc2_full).astype(jnp.bfloat16), "tensor", scatter_dimension=0, tiled=True
    ).astype(jnp.float32)
    outputs = (middle + branch + fc2_bias).astype(jnp.bfloat16)
    qkv_back, out_back, fc1_back, fc2_back = (
        lax.all_gather(qkv_weight, "dp", axis=0, tiled=True),
        lax.all_gather(out_weight, "dp", axis=1, tiled=True),
        lax.all_gather(fc1_weight, "dp", axis=0, tiled=True),
        lax.all_gather(fc2_weight, "dp", axis=1, tiled=True),
    )
    grad_outputs = cotangent.astype(jnp.float32)
    grad_branch = lax.all_gather(cotangent, "tensor", axis=0, tiled=True)
    grad_activ = jnp.einsum("rd,fd->rf", grad_branch, fc2_back, preferred_element_type=jnp.float32)
    grad_fc2 = jnp.einsum("rf,rd->fd", activ, grad_branch, preferred_element_type=jnp.float32)
    gelu_pull = jax.vjp(partial(jax.nn.gelu, approximate=True), pre_act)[1]
    grad_pre = gelu_pull(grad_activ)[0].astype(jnp.bfloat16)
    grad_fc1_b = jnp.sum(grad_pre.astype(jnp.float32), 0)
    grad_fc1 = jnp.einsum("rd,rf->df", normed2, grad_pre, preferred_element_type=jnp.float32)
    grad_normed2 = lax.psum_scatter(
        row_product_back(grad_pre, fc1_back), "tensor", scatter_dimension=0, tiled=True
    )
    norm2_pull = jax.vjp(layer_norm, middle, norm2_gain, norm2_bias)[1]
    grad_mid_norm, grad_gain2, grad_shift2 = norm2_pull(grad_normed2)
    grad_middle = grad_outputs + grad_mid_norm
    grad_attn = lax.all_gather(grad_middle.astype(jnp.bfloat16), "tensor", axis=0, tiled=True)
    grad_ctx = jnp.einsum(
        "rd,cd->rc", grad_attn, out_back, preferred_element_type=jnp.float32
    ).astype(jnp.bfloat16)
    grad_out_w = jnp.einsum("rc,rd->cd", context, grad_attn, preferred_element_type=jnp.float32)
    grad_queries, grad_keys, grad_values = lax.map(
        lambda operand: attention_backward(
            operand[0], operand[1], operand[2], operand[3], operand[4], factor
        ),
        (queries, keys, values, log_total, grad_ctx.reshape(SEQS, LEN, heads_here, HD)),
    )
    grad_proj = jnp.stack([grad_queries, grad_keys, grad_values], 3).reshape(
        total_rows, 3 * width_here
    )
    grad_qv_here = jnp.stack(
        [
            jnp.sum(grad_queries.astype(jnp.float32), (0, 1)).reshape(width_here),
            jnp.sum(grad_values.astype(jnp.float32), (0, 1)).reshape(width_here),
        ]
    )
    grad_qkv_w = jnp.einsum("rd,rc->dc", normed1, grad_proj, preferred_element_type=jnp.float32)
    grad_normed1 = lax.psum_scatter(
        row_product_back(grad_proj, qkv_back), "tensor", scatter_dimension=0, tiled=True
    )
    norm1_pull = jax.vjp(layer_norm, inputs_f, norm1_gain, norm1_bias)[1]
    grad_in_norm, grad_gain1, grad_shift1 = norm1_pull(grad_normed1)
    grad_inputs = grad_middle + grad_in_norm
    grad_qkv_s, grad_out_s, grad_fc1_s, grad_fc2_s = (
        lax.psum_scatter(grad_qkv_w, "dp", scatter_dimension=0, tiled=True),
        lax.psum_scatter(grad_out_w, "dp", scatter_dimension=1, tiled=True),
        lax.psum_scatter(grad_fc1, "dp", scatter_dimension=0, tiled=True),
        lax.psum_scatter(grad_fc2, "dp", scatter_dimension=1, tiled=True),
    )
    vector_terms = jnp.stack(
        [
            grad_gain1,
            grad_shift1,
            grad_gain2,
            grad_shift2,
            jnp.sum(grad_middle, 0),
            jnp.sum(grad_outputs, 0),
        ]
    )
    qv_whole = lax.dynamic_update_slice_in_dim(
        jnp.zeros((2, D), jnp.float32), grad_qv_here, tensor_index * width_here, 1
    )
    fc1_whole = lax.dynamic_update_slice_in_dim(
        jnp.zeros((FF,), jnp.float32), grad_fc1_b, tensor_index * hidden_here, 0
    )
    vector_sum, qv_sum, fc1_sum = lax.psum((vector_terms, qv_whole, fc1_whole), ("dp", "tensor"))
    grad_qv = lax.dynamic_slice_in_dim(qv_sum, tensor_index * width_here, width_here, 1)
    grad_fc1_bias = lax.dynamic_slice_in_dim(fc1_sum, tensor_index * hidden_here, hidden_here, 0)
    return (
        outputs,
        grad_inputs,
        vector_sum[0],
        vector_sum[1],
        grad_qkv_s,
        grad_qv,
        grad_out_s,
        vector_sum[4],
        vector_sum[2],
        vector_sum[3],
        grad_fc1_s,
        grad_fc1_bias,
        grad_fc2_s,
        vector_sum[5],
    )


ALL = ("zx", "core", "tensor")
GROUP = ("zx", "tensor")
NEG = -1e30


def natural_rows(ref, first, second, half):
    return jnp.concatenate([ref[pl.ds(first, half), :], ref[pl.ds(second, half), :]], 0)


def half_offsets(index_ref, half):
    index = index_ref[0]
    return pl.multiple_of(index * half, half), pl.multiple_of((1 - index) * half, half)


def dot_nt(left, right):
    return lax.dot_general(left, right, (((1,), (1,)), ((), ())), preferred_element_type=jnp.float32)


def dot_tn(left, right):
    return lax.dot_general(left, right, (((0,), (0,)), ((), ())), preferred_element_type=jnp.float32)


def block_probs(query_rows, keys, block):
    scores = dot_nt(query_rows, keys)
    before = keys.shape[0] - block
    rows = lax.broadcasted_iota(jnp.int32, (block, block), 0)
    columns = lax.broadcasted_iota(jnp.int32, (block, block), 1)
    diagonal = jnp.where(columns <= rows, scores[:, before:], NEG)
    if before:
        scores = jnp.concatenate([scores[:, :before], diagonal], 1)
    else:
        scores = diagonal
    expo = jnp.exp(scores - jnp.max(scores, -1, keepdims=True))
    return expo * (1.0 / jnp.sum(expo, -1, keepdims=True))


def attend_kernel(index_ref, qkv_ref, context_ref):
    half = qkv_ref.shape[0] // 2
    block = half // 2
    first, second = half_offsets(index_ref, half)
    qkv = natural_rows(qkv_ref, first, second, half)
    heads = qkv.shape[1] // (3 * HD)
    for i in range(4):
        row = (first if i < 2 else second) + (i % 2) * block
        parts = []
        for h in range(heads):
            base = h * 3 * HD
            query_rows = qkv[i * block : (i + 1) * block, base : base + HD] * HD ** (-0.5)
            keys = qkv[: (i + 1) * block, base + HD : base + 2 * HD]
            values = qkv[: (i + 1) * block, base + 2 * HD : base + 3 * HD]
            probs = block_probs(query_rows.astype(jnp.bfloat16), keys, block)
            parts.append(
                jnp.dot(probs.astype(jnp.bfloat16), values, preferred_element_type=jnp.float32)
            )
        context_ref[pl.ds(pl.multiple_of(row, block), block), :] = jnp.concatenate(
            parts, 1
        ).astype(jnp.bfloat16)


def attend_back_kernel(index_ref, qkv_ref, grad_ref, out_ref):
    half = qkv_ref.shape[0] // 2
    block = half // 2
    first, second = half_offsets(index_ref, half)
    qkv = natural_rows(qkv_ref, first, second, half)
    grad = natural_rows(grad_ref, first, second, half)
    heads = qkv.shape[1] // (3 * HD)
    starts = [
        pl.multiple_of((first if i < 2 else second) + (i % 2) * block, block) for i in range(4)
    ]
    for h in range(heads):
        base = h * 3 * HD
        queries = (qkv[:, base : base + HD] * HD ** (-0.5)).astype(jnp.bfloat16)
        keys = qkv[:, base + HD : base + 2 * HD]
        values = qkv[:, base + 2 * HD : base + 3 * HD]
        grad_head = grad[:, h * HD : (h + 1) * HD]
        grad_keys = [None] * 4
        grad_values = [None] * 4
        for i in range(4):
            rows = slice(i * block, (i + 1) * block)
            seen = slice(0, (i + 1) * block)
            probs = block_probs(queries[rows], keys[seen], block)
            grad_probs = dot_nt(grad_head[rows], values[seen])
            inner = jnp.sum(probs * grad_probs, -1, keepdims=True)
            grad_scores = (probs * (grad_probs - inner)).astype(jnp.bfloat16)
            grad_query = jnp.dot(grad_scores, keys[seen], preferred_element_type=jnp.float32)
            out_ref[pl.ds(starts[i], block), base : base + HD] = (
                grad_query * HD ** (-0.5)
            ).astype(jnp.bfloat16)
            key_term = dot_tn(grad_scores, queries[rows])
            value_term = dot_tn(probs.astype(jnp.bfloat16), grad_head[rows])
            for j in range(i + 1):
                key_part = key_term[j * block : (j + 1) * block]
                value_part = value_term[j * block : (j + 1) * block]
                grad_keys[j] = key_part if i == j else grad_keys[j] + key_part
                grad_values[j] = value_part if i == j else grad_values[j] + value_part
        for j in range(4):
            out_ref[pl.ds(starts[j], block), base + HD : base + 3 * HD] = jnp.concatenate(
                [grad_keys[j], grad_values[j]], 1
            ).astype(jnp.bfloat16)


def attend(index, qkv):
    rows, width = qkv.shape
    pairs = width // (6 * HD)
    return pl.pallas_call(
        attend_kernel,
        grid=(pairs,),
        in_specs=[
            pl.BlockSpec(memory_space=pltpu.SMEM),
            pl.BlockSpec((rows, 6 * HD), lambda i: (0, i)),
        ],
        out_specs=pl.BlockSpec((rows, 2 * HD), lambda i: (0, i)),
        out_shape=jax.ShapeDtypeStruct((rows, width // 3), jnp.bfloat16),
        compiler_params=pltpu.CompilerParams(vmem_limit_bytes=40 << 20),
        cost_estimate=pl.CostEstimate(
            flops=pairs * 8 * HD * rows * rows,
            bytes_accessed=8 * rows * width // 3,
            transcendentals=pairs * 2 * rows * rows,
        ),
    )(index, qkv)


def attend_back(index, qkv, grad):
    rows, width = qkv.shape
    pairs = width // (6 * HD)
    return pl.pallas_call(
        attend_back_kernel,
        grid=(pairs,),
        in_specs=[
            pl.BlockSpec(memory_space=pltpu.SMEM),
            pl.BlockSpec((rows, 6 * HD), lambda i: (0, i)),
            pl.BlockSpec((rows, 2 * HD), lambda i: (0, i)),
        ],
        out_specs=pl.BlockSpec((rows, 6 * HD), lambda i: (0, i)),
        out_shape=jax.ShapeDtypeStruct((rows, width), jnp.bfloat16),
        compiler_params=pltpu.CompilerParams(vmem_limit_bytes=40 << 20),
        cost_estimate=pl.CostEstimate(
            flops=pairs * 20 * HD * rows * rows,
            bytes_accessed=14 * rows * width // 3,
            transcendentals=pairs * 2 * rows * rows,
        ),
    )(index, qkv, grad)


def pair_body(
    zx_size,
    inputs,
    norm1_gain,
    norm1_bias,
    qkv_weight,
    qv_bias,
    out_weight,
    out_bias,
    norm2_gain,
    norm2_bias,
    fc1_weight,
    fc1_bias,
    fc2_weight,
    fc2_bias,
    cotangent,
):
    f32, bf16 = jnp.float32, jnp.bfloat16
    crossing = [
        (z * 4 + c * 2 + t, z * 4 + t * 2 + c)
        for z in range(zx_size)
        for c in range(2)
        for t in range(2)
    ]

    def swap(value):
        return lax.ppermute(value, ALL, crossing)

    def flip(value):
        return lax.ppermute(value, "core", [(0, 1), (1, 0)])

    def both(own):
        return jnp.concatenate([own, flip(own)], 0)

    def pair_sum(product, rows):
        half = rows.shape[0] // 2
        arrived = flip(product(rows[half:]).astype(bf16))
        return product(rows[:half]) + arrived.astype(f32)

    levels = zx_size.bit_length() - 1
    zx_index, tensor_index = lax.axis_index("zx"), lax.axis_index("tensor")

    def bit_of(d):
        return tensor_index if d == levels else (zx_index // 2 ** (levels - 1 - d)) % 2

    def across(value, d):
        if d == levels:
            return lax.ppermute(value, "tensor", [(0, 1), (1, 0)])
        distance = 2 ** (levels - 1 - d)
        return lax.ppermute(value, "zx", [(i, i ^ distance) for i in range(zx_size)])

    def order_of(last):
        return [d for d in range(levels + 1) if d != last] + [last]

    def gather(weight, last):
        block = weight.shape
        held = weight.reshape((1,) * (levels + 1) + block)
        for d in order_of(last):
            other = across(held, d)
            held = jnp.where(
                bit_of(d) == 0,
                jnp.concatenate([held, other], d),
                jnp.concatenate([other, held], d),
            )
        return held.reshape(-1, block[1])

    def scatter(grad, last):
        rows, columns = grad.shape
        held = grad.reshape((2,) * (levels + 1) + (rows // (2 * zx_size), columns))
        for d in reversed(order_of(last)):
            bit = bit_of(d)
            other = across(lax.dynamic_slice_in_dim(held, 1 - bit, 1, d), d)
            kept = lax.dynamic_slice_in_dim(held, bit, 1, d)
            held = (kept.astype(f32) + other.astype(f32)).astype(bf16)
        return swap(held.reshape(-1, columns)).astype(f32)

    def product_tn(left, right):
        return jnp.einsum("ra,rb->ab", left, right, preferred_element_type=f32).astype(bf16)

    inputs = swap(inputs)
    qkv_full = gather(swap(qkv_weight), levels - 1)
    qv_bias = swap(qv_bias)
    fc1_bias = swap(fc1_bias)
    out_turned = gather(swap(out_weight.T), levels)
    fc1_full = gather(swap(fc1_weight), levels)
    fc2_turned = gather(swap(fc2_weight.T), levels - 2)
    cotangent = swap(cotangent)

    width_here = qv_bias.shape[1]
    heads_here = width_here // HD
    inputs_f = inputs.astype(f32)
    index = lax.axis_index("core").astype(jnp.int32).reshape(1)
    normed1 = both(layer_norm(inputs_f, norm1_gain, norm1_bias).astype(bf16))
    head_bias = jnp.stack(
        [
            qv_bias[0].reshape(heads_here, HD),
            jnp.zeros((heads_here, HD), f32),
            qv_bias[1].reshape(heads_here, HD),
        ],
        1,
    ).reshape(3 * width_here)
    qkv = (row_product(normed1, qkv_full) + head_bias).astype(bf16)
    context = attend(index, qkv)
    middle = inputs_f + pair_sum(lambda rows: row_product_back(rows, out_turned), context) + out_bias
    normed2 = both(layer_norm(middle, norm2_gain, norm2_bias).astype(bf16))
    pre_act = row_product(normed2, fc1_full) + fc1_bias
    activ = jax.nn.gelu(pre_act, approximate=True).astype(bf16)
    branch = pair_sum(lambda rows: row_product_back(rows, fc2_turned), activ)
    outputs = swap((middle + branch + fc2_bias).astype(bf16))

    grad_outputs = cotangent.astype(f32)
    grad_branch = both(cotangent)
    grad_fc2_part = product_tn(grad_branch, activ)
    grad_fc2_part, grad_branch = lax.optimization_barrier((grad_fc2_part, grad_branch))
    grad_fc2 = scatter(grad_fc2_part, levels - 2).T
    grad_activ = row_product(grad_branch, fc2_turned)
    gelu_pull = jax.vjp(partial(jax.nn.gelu, approximate=True), pre_act)[1]
    grad_pre = gelu_pull(grad_activ)[0].astype(bf16)
    grad_fc1_b = jnp.sum(grad_pre.astype(f32), 0)
    grad_fc1_part = product_tn(normed2, grad_pre)
    grad_fc1_part, grad_pre = lax.optimization_barrier((grad_fc1_part, grad_pre))
    grad_fc1 = scatter(grad_fc1_part, levels)
    grad_normed2 = pair_sum(lambda rows: row_product_back(rows, fc1_full), grad_pre)
    norm2_pull = jax.vjp(layer_norm, middle, norm2_gain, norm2_bias)[1]
    grad_mid_norm, grad_gain2, grad_shift2 = norm2_pull(grad_normed2)
    grad_middle = grad_outputs + grad_mid_norm
    grad_attn = both(grad_middle.astype(bf16))
    grad_out_part = product_tn(grad_attn, context)
    grad_out_part, grad_attn = lax.optimization_barrier((grad_out_part, grad_attn))
    grad_out = scatter(grad_out_part, levels).T
    grad_ctx = row_product(grad_attn, out_turned).astype(bf16)
    grad_proj = attend_back(index, qkv, grad_ctx)
    grad_bias = jnp.sum(grad_proj.astype(f32), 0).reshape(heads_here, 3, HD)
    grad_qkv_part = product_tn(normed1, grad_proj)
    grad_qkv_part, grad_proj = lax.optimization_barrier((grad_qkv_part, grad_proj))
    grad_qkv = scatter(grad_qkv_part, levels - 1)
    grad_normed1 = pair_sum(lambda rows: row_product_back(rows, qkv_full), grad_proj)
    norm1_pull = jax.vjp(layer_norm, inputs_f, norm1_gain, norm1_bias)[1]
    grad_in_norm, grad_gain1, grad_shift1 = norm1_pull(grad_normed1)
    grad_inputs = swap((grad_middle + grad_in_norm).astype(bf16)).astype(f32)

    vectors = [
        grad_gain1,
        grad_shift1,
        grad_gain2,
        grad_shift2,
        jnp.sum(grad_middle, 0),
        jnp.sum(grad_outputs, 0),
    ]
    width = inputs.shape[1]
    hidden = grad_fc1_b.shape[0]
    terms = jnp.concatenate(
        vectors + [grad_bias[:, 0].reshape(-1), grad_bias[:, 2].reshape(-1), grad_fc1_b]
    )
    gathered = lax.all_gather(terms, ALL, axis=0, tiled=False)
    gathered = gathered.reshape(zx_size, 2, 2, terms.shape[0])
    common = jnp.sum(gathered[..., : 6 * width], (0, 1, 2)).reshape(6, width)
    halves = jnp.sum(gathered[..., 6 * width :], (0, 2))
    mine = lax.dynamic_index_in_dim(halves, lax.axis_index("tensor"), 0, False)
    return (
        outputs,
        grad_inputs,
        common[0],
        common[1],
        grad_qkv,
        mine[: 2 * width_here].reshape(2, width_here),
        grad_out,
        common[4],
        common[2],
        common[3],
        grad_fc1,
        mine[2 * width_here : 2 * width_here + hidden],
        grad_fc2,
        common[5],
    )


def pair_solution(mesh):
    zx_size = mesh.shape["dp"] // 2
    split = Mesh(mesh.devices.reshape(zx_size, 2, 2), ALL)
    rows, spread = P(ALL, None), ("zx", "core")
    return jax.shard_map(
        partial(pair_body, zx_size),
        mesh=split,
        in_specs=(
            rows,
            P(),
            P(),
            P(spread, "tensor"),
            P(None, "tensor"),
            P("tensor", spread),
            P(),
            P(),
            P(),
            P(spread, "tensor"),
            P("tensor"),
            P("tensor", spread),
            P(),
            rows,
        ),
        out_specs=(
            rows,
            rows,
            P(),
            P(),
            P(spread, "tensor"),
            P(None, "tensor"),
            P("tensor", spread),
            P(),
            P(),
            P(),
            P(spread, "tensor"),
            P("tensor"),
            P("tensor", spread),
            P(),
        ),
        check_vma=False,
    )


def solution(mesh):
    dp_size = mesh.shape["dp"]
    if mesh.shape["tensor"] == 2 and dp_size >= 8 and dp_size & (dp_size - 1) == 0:
        return pair_solution(mesh)
    placed = (
        P(("dp", "tensor"), None),
        P(),
        P(),
        P("dp", "tensor"),
        P(None, "tensor"),
        P("tensor", "dp"),
        P(),
        P(),
        P(),
        P("dp", "tensor"),
        P("tensor"),
        P("tensor", "dp"),
        P(),
        P(("dp", "tensor"), None),
    )
    return jax.shard_map(
        body,
        mesh=mesh,
        in_specs=placed,
        out_specs=(
            P(("dp", "tensor"), None),
            P(("dp", "tensor"), None),
            P(),
            P(),
            P("dp", "tensor"),
            P(None, "tensor"),
            P("tensor", "dp"),
            P(),
            P(),
            P(),
            P("dp", "tensor"),
            P("tensor"),
            P("tensor", "dp"),
            P(),
        ),
        check_vma=False,
    )
```
